32 devices in a mesh: seq: 2 (over core), ctx: 16 (over z, y, x).
Axes of the slice: x: 2, y: 2, z: 4, core: 2. Of those that a mesh axis runs over, the one named last changes fastest.
Arguments:
- layer_input: bfloat16 [2, 4096, 1024], P('seq', 'ctx'), may hold values from -6 to 6
- ln1_gain: bfloat16 [1024], P('seq'), may hold values from 0.5 to 1.5
- ln1_bias: bfloat16 [1024], P('seq'), may hold values from -3 to 3
- qkv_weight: bfloat16 [1024, 3072], P('seq'), may hold values from -0.1875 to 0.1875
- query_bias: bfloat16 [1024], P('seq'), may hold values from -3 to 3
- value_bias: bfloat16 [1024], P('seq'), may hold values from -3 to 3
- out_weight: bfloat16 [1024, 1024], P('seq'), may hold values from -0.75 to 0.75
- out_bias: bfloat16 [1024], P('seq'), may hold values from -3 to 3
- ln2_gain: bfloat16 [1024], P('seq'), may hold values from 0.5 to 1.5
- ln2_bias: bfloat16 [1024], P('seq'), may hold values from -3 to 3
- up_weight: bfloat16 [1024, 4096], P('seq'), may hold values from -0.1875 to 0.1875
- up_bias: bfloat16 [4096], P('seq'), may hold values from -3 to 3
- down_weight: bfloat16 [4096, 1024], P('seq'), may hold values from -0.09375 to 0.09375
- down_bias: bfloat16 [1024], P('seq'), may hold values from -3 to 3
- out_cotangent: bfloat16 [2, 4096, 1024], P('seq', 'ctx'), may hold values from -6 to 6
Outputs:
- layer_output: bfloat16 [2, 4096, 1024], P('seq', 'ctx')
- input_grad: float32 [2, 4096, 1024], P('seq', 'ctx')
- ln1_gain_grad: float32 [1024], P('seq')
- ln1_bias_grad: float32 [1024], P('seq')
- qkv_weight_grad: float32 [1024, 3072], P('seq')
- query_bias_grad: float32 [1024], P('seq')
- value_bias_grad: float32 [1024], P('seq')
- out_weight_grad: float32 [1024, 1024], P('seq')
- out_bias_grad: float32 [1024], P('seq')
- ln2_gain_grad: float32 [1024], P('seq')
- ln2_bias_grad: float32 [1024], P('seq')
- up_weight_grad: float32 [1024, 4096], P('seq')
- up_bias_grad: float32 [4096], P('seq')
- down_weight_grad: float32 [4096, 1024], P('seq')
- down_bias_grad: float32 [1024], P('seq')
The draws below stay inside these ranges and needn't reach their ends.
All inputs are finite; a program needn't handle non-finite values.
Results may differ from the reference program's by a relative error of at most 0.035.
Values may be sent and summed in bfloat16 or wider, within the bound.
A program may use at most 256 MiB of HBM per device.

```python
import jax
import jax.numpy as jnp
from jax import lax

D = 1024
HEADS = 16
HEAD_DIM = 64
FF = 4096
SEQS = 2
LENGTH = 4096


def block_scale(rng, extent, cuts, least, largest):
    factor_of, own = 1.0, jax.random.fold_in(rng, 6)
    for axis_at, blocks in cuts:
        draws = jnp.exp(jax.random.uniform(jax.random.fold_in(own, axis_at), (blocks,), jnp.float32, least / len(cuts), largest / len(cuts)))
        factor_of = factor_of * jnp.repeat(draws, extent[axis_at] // blocks).reshape([-1 if axis == axis_at else 1 for axis in range(len(extent))])
    return factor_of


def normal_values(stream_key, shape, deviation, most, cuts=(), kind=jnp.bfloat16):
    level = block_scale(stream_key, shape, cuts, -0.22, 0.18) if cuts else 1.0
    drawn = jax.random.normal(stream_key, shape, jnp.float32) * deviation * level
    return jnp.minimum(jnp.maximum(drawn, -most), most).astype(kind)


def setup_inputs(seed: int = 0) -> dict:
    key_of = jax.random.split(jax.random.key(seed), 16)
    layer_input = normal_values(key_of[0], (SEQS, LENGTH, D), 1.0, 6.0, ((0, 2), (1, 16)))
    ln1_gain = jnp.clip(1.0 + 0.1 * jax.random.normal(key_of[1], (D,), jnp.float32), 0.5, 1.5).astype(jnp.bfloat16)
    ln1_bias = normal_values(key_of[2], (D,), 0.5, 3.0, ((0, 2),))
    qkv_weight = normal_values(key_of[3], (D, 3 * D), D ** -0.5, 0.1875, ((0, 2),))
    query_bias = normal_values(key_of[4], (D,), 0.5, 3.0, ((0, 2),))
    value_bias = normal_values(key_of[5], (D,), 0.5, 3.0, ((0, 2),))
    out_weight = normal_values(key_of[6], (D, D), (D // 16) ** -0.5, 0.75, ((0, 2),))
    out_bias = normal_values(key_of[7], (D,), 0.5, 3.0, ((0, 2),))
    ln2_gain = jnp.clip(1.0 + 0.1 * jax.random.normal(key_of[8], (D,), jnp.float32), 0.5, 1.5).astype(jnp.bfloat16)
    ln2_bias = normal_values(key_of[9], (D,), 0.5, 3.0, ((0, 2),))
    up_weight = normal_values(key_of[10], (D, FF), D ** -0.5, 0.1875, ((0, 2),))
    up_bias = normal_values(key_of[11], (FF,), 0.5, 3.0, ((0, 2),))
    down_weight = normal_values(key_of[12], (FF, D), FF ** -0.5, 0.09375, ((0, 2),))
    down_bias = normal_values(key_of[13], (D,), 0.5, 3.0, ((0, 2),))
    out_cotangent = normal_values(key_of[14], (SEQS, LENGTH, D), 1.0, 6.0, ((0, 2), (1, 16)))
    return dict(layer_input=layer_input, ln1_gain=ln1_gain, ln1_bias=ln1_bias, qkv_weight=qkv_weight, query_bias=query_bias, value_bias=value_bias, out_weight=out_weight, out_bias=out_bias, ln2_gain=ln2_gain, ln2_bias=ln2_bias, up_weight=up_weight, up_bias=up_bias, down_weight=down_weight, down_bias=down_bias, out_cotangent=out_cotangent)


EPS = 1e-05
FLOOR_SCORE = -1e+30

@jax.custom_vjp
def low(v):
    return lax.optimization_barrier(v.astype(jnp.bfloat16)).astype(jnp.float32)

@jax.custom_vjp
def low_back(v):
    return v

def low_keep(v):
    return (low(v), None)

def low_pass(kept, grad):
    return (grad,)

def back_keep(v):
    return (v, None)

def back_low(kept, grad):
    return (low(grad),)
low.defvjp(low_keep, low_pass)
low_back.defvjp(back_keep, back_low)

def layer_norm(values, gain, shift):
    centre = values - lax.optimization_barrier(jnp.mean(values, axis=-1, keepdims=True))
    spread = lax.optimization_barrier(jnp.mean(centre * centre, axis=-1, keepdims=True))
    return centre * lax.rsqrt(spread + EPS) * gain + shift

def attend(queries, keys, values):
    length = queries.shape[0]
    block_rows = min(512, length)
    blocks = length // block_rows
    query_blocks = queries.reshape(blocks, block_rows, HEADS, HEAD_DIM)
    key_heads = keys.reshape(length, HEADS, HEAD_DIM)
    value_heads = values.reshape(length, HEADS, HEAD_DIM)
    offsets = jnp.arange(blocks, dtype=jnp.int32) * block_rows

    def one_block(pair):
        query_block, offset = pair
        scores = jnp.einsum('qhd,khd->hqk', query_block, key_heads, precision=lax.Precision.HIGHEST) * HEAD_DIM ** (-0.5)
        scores = low_back(scores)
        query_pos = offset + jnp.arange(block_rows, dtype=jnp.int32)
        key_pos = jnp.arange(length, dtype=jnp.int32)
        allowed = key_pos[None, :] <= query_pos[:, None]
        scores = jnp.where(allowed, scores, FLOOR_SCORE)
        top = lax.optimization_barrier(jnp.max(scores, axis=-1, keepdims=True))
        weights = jnp.where(allowed, jnp.exp(scores - top), 0.0)
        probs = weights / lax.optimization_barrier(jnp.sum(weights, axis=-1, keepdims=True))
        mixed = jnp.einsum('hqk,khd->qhd', low(probs), value_heads, precision=lax.Precision.HIGHEST)
        return mixed.reshape(block_rows, HEADS * HEAD_DIM)
    outputs = lax.map(jax.checkpoint(one_block), (query_blocks, offsets))
    return outputs.reshape(length, HEADS * HEAD_DIM)

def layer(params, inputs):
    gain_one, shift_one, qkv_w, q_bias, v_bias, out_w, o_bias, gain_two, shift_two, up_w, u_bias, down_w, d_bias = params
    highest = lax.Precision.HIGHEST
    normed_one = low(layer_norm(inputs, gain_one, shift_one))
    projected = jnp.dot(normed_one, qkv_w, precision=highest, preferred_element_type=jnp.float32)
    queries = low(low_back(projected[:, :D] + q_bias))
    keys = low(low_back(projected[:, D:2 * D]))
    values = low(low_back(projected[:, 2 * D:] + v_bias))
    attention = low(low_back(attend(queries, keys, values)))
    mid = inputs + low_back(jnp.dot(attention, out_w, precision=highest, preferred_element_type=jnp.float32) + o_bias)
    normed_two = low(layer_norm(mid, gain_two, shift_two))
    hidden = low_back(jnp.dot(normed_two, up_w, precision=highest, preferred_element_type=jnp.float32) + u_bias)
    activated = low(jax.nn.gelu(hidden))
    return mid + jnp.dot(activated, down_w, precision=highest, preferred_element_type=jnp.float32) + d_bias

def reference(layer_input, ln1_gain, ln1_bias, qkv_weight, query_bias, value_bias, out_weight, out_bias, ln2_gain, ln2_bias, up_weight, up_bias, down_weight, down_bias, out_cotangent):
    params = tuple((p.astype(jnp.float32) for p in (ln1_gain, ln1_bias, qkv_weight, query_bias, value_bias, out_weight, out_bias, ln2_gain, ln2_bias, up_weight, up_bias, down_weight, down_bias)))
    inputs_all = layer_input.astype(jnp.float32)
    cotangents = out_cotangent.astype(jnp.float32)

    def one_sequence(totals, item):
        inputs, cotangent = item
        result, pull = jax.vjp(layer, params, inputs)
        param_grads, input_grads = pull(cotangent)
        totals = tuple((a + b for a, b in zip(totals, param_grads)))
        return (totals, (result.astype(jnp.bfloat16), input_grads))
    zeros = tuple((jnp.zeros_like(p) for p in params))
    totals, (outputs, input_grads) = lax.scan(one_sequence, zeros, (inputs_all, cotangents))
    return (outputs, input_grads, totals[0], totals[1], totals[2], totals[3], totals[4], totals[5], totals[6], totals[7], totals[8], totals[9], totals[10], totals[11], totals[12])
```

```python
import functools
import math

import jax
import jax.numpy as jnp
from jax import lax
from jax.experimental import pallas as pl
from jax.experimental.pallas import tpu as pltpu
from jax.sharding import PartitionSpec as P

HEADS = 16
HEAD_DIM = 64


EPS = 1e-05
FLOOR_SCORE = -1e30
UNIT_ROWS = 16


def layer_norm(values, gain, shift):
    centre = values - jnp.mean(values, axis=-1, keepdims=True)
    spread = jnp.mean(centre * centre, axis=-1, keepdims=True)
    return centre * lax.rsqrt(spread + EPS) * gain + shift


def split_heads(values):
    return values.reshape(values.shape[0], values.shape[1], HEADS, HEAD_DIM)


def causal(query_first, query_rows, key_first, key_rows):
    query_pos = query_first + jnp.arange(query_rows, dtype=jnp.int32)
    key_pos = key_first + jnp.arange(key_rows, dtype=jnp.int32)
    return key_pos[None, :] <= query_pos[:, None]


def over_blocks(running, arrays, advance):
    piece_rows = arrays[0].shape[1]
    block_rows = math.gcd(piece_rows, 512)
    pieces = piece_rows // block_rows
    stacked = tuple(
        (
            jnp.moveaxis(item.reshape(item.shape[:1] + (pieces, block_rows) + item.shape[2:]), 1, 0)
            for item in arrays
        )
    )

    def inner(kept, pair):
        blocks, position = pair
        return (advance(kept, blocks, position * block_rows), None)

    result, unused = lax.scan(inner, running, (stacked, jnp.arange(pieces, dtype=jnp.int32)))
    return result


def dot(left, right, left_axis=1, right_axis=0):
    return lax.dot_general(
        left, right, (((left_axis,), (right_axis,)), ((), ())), preferred_element_type=jnp.float32
    )


def diagonal(rows):
    key_at = lax.broadcasted_iota(jnp.int32, (rows, rows), 0)
    query_at = lax.broadcasted_iota(jnp.int32, (rows, rows), 1)
    return key_at <= query_at


def forward_kernel(rows, query_ref, key_ref, value_ref, out_ref, log_ref):
    at = pl.program_id(1)
    query = query_ref[0]

    def advance(block, kept, masked):
        top, total, accum = kept
        first = pl.multiple_of(block * rows, rows)
        scores = dot(key_ref[0, pl.ds(first, rows), :], query)
        if masked:
            scores = jnp.where(diagonal(rows), scores, FLOOR_SCORE)
        new_top = jnp.maximum(top, jnp.max(scores, axis=0, keepdims=True))
        weights = jnp.exp(scores - new_top)
        factor = jnp.exp(top - new_top)
        total = total * factor + jnp.sum(weights, axis=0, keepdims=True)
        mixed = dot(value_ref[0, :, pl.ds(first, rows)], weights.astype(jnp.bfloat16))
        return new_top, total, accum * factor + mixed

    state = (
        jnp.full((1, rows), FLOOR_SCORE, jnp.float32),
        jnp.zeros((1, rows), jnp.float32),
        jnp.zeros((HEAD_DIM, rows), jnp.float32),
    )
    state = lax.fori_loop(0, at, lambda block, kept: advance(block, kept, False), state)
    top, total, accum = advance(at, state, True)
    out_ref[0] = accum / total
    log_ref[0] = top + jnp.log(total)


def attend(query_t, key, value_t, rows):
    batch, features, length = query_t.shape
    pairs = batch * length * (length + rows) // 2
    return pl.pallas_call(
        functools.partial(forward_kernel, rows),
        grid=(batch, length // rows),
        in_specs=[
            pl.BlockSpec((1, features, rows), lambda b, i: (b, 0, i)),
            pl.BlockSpec((1, length, features), lambda b, i: (b, 0, 0)),
            pl.BlockSpec((1, features, length), lambda b, i: (b, 0, 0)),
        ],
        out_specs=[
            pl.BlockSpec((1, features, rows), lambda b, i: (b, 0, i)),
            pl.BlockSpec((1, 1, rows), lambda b, i: (b, 0, i)),
        ],
        out_shape=[
            jax.ShapeDtypeStruct((batch, features, length), jnp.float32),
            jax.ShapeDtypeStruct((batch, 1, length), jnp.float32),
        ],
        compiler_params=pltpu.CompilerParams(vmem_limit_bytes=48 * 2**20),
        cost_estimate=pl.CostEstimate(
            flops=4 * features * pairs, bytes_accessed=16 * features * length, transcendentals=pairs
        ),
    )(query_t, key, value_t)


def backward_kernel(
    rows,
    query_ref,
    query_t_ref,
    key_ref,
    key_t_ref,
    value_ref,
    grad_ref,
    grad_t_ref,
    log_ref,
    delta_ref,
    query_grad_ref,
    key_grad_ref,
    value_grad_ref,
    query_acc,
):
    at = pl.program_id(1)
    blocks = pl.num_programs(1)
    key = key_ref[0]
    key_t = key_t_ref[0]
    value = value_ref[0]

    @pl.when(at == 0)
    def clear():
        query_acc[...] = jnp.zeros_like(query_acc)

    def advance(block, kept, masked):
        key_sum, value_sum = kept
        first = pl.multiple_of(block * rows, rows)
        part = pl.ds(first, rows)
        scores = dot(key, query_t_ref[0, :, part])
        probs = jnp.exp(scores - log_ref[0, :, part])
        if masked:
            probs = jnp.where(diagonal(rows), probs, 0.0)
        prob_grad = dot(value, grad_t_ref[0, :, part])
        score_grad = (probs * (prob_grad - delta_ref[0, :, part])).astype(jnp.bfloat16)
        value_sum = value_sum + dot(probs.astype(jnp.bfloat16), grad_ref[0, part, :])
        key_sum = key_sum + dot(score_grad, query_ref[0, part, :])
        query_acc[:, part] += dot(key_t, score_grad)
        return key_sum, value_sum

    zero = jnp.zeros((rows, HEAD_DIM), jnp.float32)
    state = advance(at, (zero, zero), True)
    key_sum, value_sum = lax.fori_loop(
        at + 1, blocks, lambda block, kept: advance(block, kept, False), state
    )
    key_grad_ref[0] = key_sum.T.astype(jnp.bfloat16)
    value_grad_ref[0] = value_sum.T.astype(jnp.bfloat16)

    @pl.when(at == blocks - 1)
    def finish():
        query_grad_ref[0] = (query_acc[...] * HEAD_DIM**-0.5).astype(jnp.bfloat16)


def attend_back(query, query_t, key, key_t, value, grad, grad_t, log_total, delta, rows):
    batch, features, length = query_t.shape
    pairs = batch * length * (length + rows) // 2
    whole = pl.BlockSpec((1, length, features), lambda b, j: (b, 0, 0))
    whole_t = pl.BlockSpec((1, features, length), lambda b, j: (b, 0, 0))
    piece = pl.BlockSpec((1, rows, features), lambda b, j: (b, j, 0))
    piece_t = pl.BlockSpec((1, features, rows), lambda b, j: (b, 0, j))
    line = pl.BlockSpec((1, 1, length), lambda b, j: (b, 0, 0))
    shape = jax.ShapeDtypeStruct((batch, features, length), jnp.bfloat16)
    return pl.pallas_call(
        functools.partial(backward_kernel, rows),
        grid=(batch, length // rows),
        in_specs=[whole, whole_t, piece, piece_t, piece, whole, whole_t, line, line],
        out_specs=[whole_t, piece_t, piece_t],
        out_shape=[shape, shape, shape],
        scratch_shapes=[pltpu.VMEM((features, length), jnp.float32)],
        compiler_params=pltpu.CompilerParams(vmem_limit_bytes=48 * 2**20),
        cost_estimate=pl.CostEstimate(
            flops=10 * features * pairs, bytes_accessed=24 * features * length, transcendentals=pairs
        ),
    )(query, query_t, key, key_t, value, grad, grad_t, log_total, delta)


def to_heads(values_t, ways):
    seqs, parts, width, rows = values_t.shape
    own = HEADS // ways
    cut = values_t.reshape(seqs, parts, ways, own, HEAD_DIM, rows)
    cut = jnp.transpose(cut, (2, 1, 0, 3, 4, 5))
    moved = lax.all_to_all(cut, "ctx", 0, 0)
    joined = jnp.transpose(moved, (1, 2, 3, 4, 0, 5))
    return joined.reshape(parts, seqs * own, HEAD_DIM, ways * rows)


def to_positions(values_t, ways, seqs):
    parts, batch, features, length = values_t.shape
    own = HEADS // ways
    cut = values_t.reshape(parts, seqs, own, features, ways, length // ways)
    cut = jnp.transpose(cut, (4, 0, 1, 2, 3, 5))
    moved = lax.all_to_all(cut, "ctx", 0, 0)
    joined = jnp.transpose(moved, (2, 1, 0, 3, 4, 5))
    return joined.reshape(seqs, parts, HEADS * HEAD_DIM, length // ways)


def head_forward(queries, keys, values):
    ways = lax.axis_size("ctx")
    scale = jnp.asarray(HEAD_DIM**-0.5, jnp.bfloat16)
    stacked = jnp.stack([queries * scale, keys, values], axis=1)
    query_t, key_t, value_t = to_heads(jnp.swapaxes(stacked, 2, 3), ways)
    rows = math.gcd(query_t.shape[2], 512)
    key = jnp.swapaxes(key_t, 1, 2)
    out_t, log_total = attend(query_t, key, value_t, rows)
    low_t = to_positions(out_t[None].astype(jnp.bfloat16), ways, queries.shape[0])[:, 0]
    return jnp.swapaxes(low_t, 1, 2), (query_t, key, key_t, value_t, out_t, log_total)


def head_backward(kept, attention_grad, parts):
    query_t, key, key_t, value_t, out_t, log_total = kept
    ways = lax.axis_size("ctx")
    seqs = attention_grad.shape[0]
    (grad_t,) = to_heads(jnp.swapaxes(attention_grad, 1, 2)[:, None], ways)
    delta = jnp.sum(grad_t.astype(jnp.float32) * out_t, axis=1, keepdims=True)
    operands = (
        jnp.swapaxes(query_t, 1, 2),
        query_t,
        key,
        key_t,
        jnp.swapaxes(value_t, 1, 2),
        jnp.swapaxes(grad_t, 1, 2),
        grad_t,
        log_total,
        delta,
    )
    rows = math.gcd(query_t.shape[2], 512)
    if query_t.shape[0] == 1 and can_sum(parts):
        grads, sums = attend_back_sum(0, operands, parts, rows)
    else:
        grads = attend_back(*operands, rows)
        sums = total_grads(0, parts)
    back = to_positions(jnp.stack(grads), ways, seqs)
    return [jnp.swapaxes(back[:, at], 1, 2) for at in range(3)], sums


def block_forward(queries, keys, values):
    seq_count, block_len, model_width = queries.shape
    scale_factor = HEAD_DIM ** (-0.5)
    my_start = lax.axis_index("ctx") * block_len
    f32 = jnp.float32
    bf16 = jnp.bfloat16
    query_heads = split_heads(queries)

    def forward_block(running, blocks, key_start):
        key_block, value_block = blocks
        key_rows = key_block.shape[1]

        def forward_compute(kept):
            top, total, accum = kept
            allowed = causal(my_start, block_len, key_start, key_rows)
            scores = (
                jnp.einsum(
                    "sqhd,skhd->shqk",
                    query_heads,
                    split_heads(key_block),
                    preferred_element_type=f32,
                )
                * scale_factor
            )
            scores = jnp.where(allowed, scores, FLOOR_SCORE)
            new_top = jnp.maximum(top, jnp.max(scores, axis=-1))
            factor = jnp.exp(top - new_top)
            weights = jnp.where(allowed, jnp.exp(scores - new_top[..., None]), 0.0)
            new_total = total * factor + jnp.sum(weights, axis=-1)
            mixed = jnp.einsum(
                "shqk,skhd->sqhd",
                weights.astype(bf16),
                split_heads(value_block),
                preferred_element_type=f32,
            )
            new_accum = accum * jnp.transpose(factor, (0, 2, 1))[..., None] + mixed
            return (new_top, new_total, new_accum)

        return lax.cond(
            key_start > my_start + block_len - 1, lambda kept: kept, forward_compute, running
        )

    start_state = (
        jnp.full((seq_count, HEADS, block_len), FLOOR_SCORE, f32),
        jnp.zeros((seq_count, HEADS, block_len), f32),
        jnp.zeros((seq_count, block_len, HEADS, HEAD_DIM), f32),
    )
    top, total, accum = over_blocks(
        start_state,
        (
            lax.all_gather(keys, "ctx", axis=1, tiled=True),
            lax.all_gather(values, "ctx", axis=1, tiled=True),
        ),
        forward_block,
    )
    attention = (accum / jnp.transpose(total, (0, 2, 1))[..., None]).reshape(
        seq_count, block_len, model_width
    )
    log_total = top + jnp.log(total)
    return attention, log_total


def block_backward(queries, keys, values, attention, log_total, attention_grad):
    seq_count, block_len, model_width = queries.shape
    scale_factor = HEAD_DIM ** (-0.5)
    my_start = lax.axis_index("ctx") * block_len
    f32 = jnp.float32
    bf16 = jnp.bfloat16
    query_heads = split_heads(queries)

    grad_heads = split_heads(attention_grad)
    delta_rows = jnp.sum(split_heads(attention_grad.astype(f32) * attention), axis=-1)
    delta_heads = jnp.transpose(delta_rows, (0, 2, 1))

    def keys_block(running, blocks, key_start):
        key_block, value_block = blocks
        key_rows = key_block.shape[1]

        def keys_compute(kept):
            query_acc, key_grads, value_grads = kept
            allowed = causal(my_start, block_len, key_start, key_rows)
            block_keys = split_heads(key_block)
            scores = (
                jnp.einsum("sqhd,skhd->shqk", query_heads, block_keys, preferred_element_type=f32)
                * scale_factor
            )
            probs = jnp.where(allowed, jnp.exp(scores - log_total[..., None]), 0.0)
            prob_grad = jnp.einsum(
                "sqhd,skhd->shqk", grad_heads, split_heads(value_block), preferred_element_type=f32
            )
            score_grad = (probs * (prob_grad - delta_heads[..., None])).astype(bf16)
            query_acc = (
                query_acc
                + jnp.einsum("shqk,skhd->sqhd", score_grad, block_keys, preferred_element_type=f32)
                * scale_factor
            )
            key_term = (
                jnp.einsum("shqk,sqhd->skhd", score_grad, query_heads, preferred_element_type=f32)
                * scale_factor
            ).reshape(seq_count, key_rows, model_width)
            value_term = jnp.einsum(
                "shqk,sqhd->skhd", probs.astype(bf16), grad_heads, preferred_element_type=f32
            ).reshape(seq_count, key_rows, model_width)
            key_grads = lax.dynamic_update_slice_in_dim(key_grads, key_term, key_start, 1)
            value_grads = lax.dynamic_update_slice_in_dim(value_grads, value_term, key_start, 1)
            return (query_acc, key_grads, value_grads)

        return lax.cond(
            key_start > my_start + block_len - 1, lambda kept: kept, keys_compute, running
        )

    whole_len = block_len * lax.axis_size("ctx")
    keys_state = (
        jnp.zeros((seq_count, block_len, HEADS, HEAD_DIM), f32),
        jnp.zeros((seq_count, whole_len, model_width), f32),
        jnp.zeros((seq_count, whole_len, model_width), f32),
    )
    query_acc, key_grads, value_grads = over_blocks(
        keys_state,
        (
            lax.all_gather(keys, "ctx", axis=1, tiled=True),
            lax.all_gather(values, "ctx", axis=1, tiled=True),
        ),
        keys_block,
    )
    query_sum = query_acc.reshape(seq_count, block_len, model_width)
    key_sum, value_sum = (
        lax.psum_scatter(
            key_grads.astype(jnp.bfloat16), "ctx", scatter_dimension=1, tiled=True
        ).astype(jnp.float32),
        lax.psum_scatter(
            value_grads.astype(jnp.bfloat16), "ctx", scatter_dimension=1, tiled=True
        ).astype(jnp.float32),
    )
    return query_sum.astype(bf16), key_sum.astype(bf16), value_sum.astype(bf16)


def total_grad(part):
    owned = lax.psum_scatter(part.astype(jnp.bfloat16), "seq", scatter_dimension=0, tiled=True)
    return lax.psum(owned, "ctx").astype(jnp.float32)


MESH = pl.DeviceIdType.MESH


def sum_plan(sizes, ways, unit_cols, refs):
    count = len(sizes)
    parts, outs = refs[:count], refs[count : 2 * count]
    own, far, near, kept, here_sem, far_send, far_recv, send, recv, back_send, back_recv = refs[
        2 * count :
    ]
    unit_rows = UNIT_ROWS * ways
    bits = [2**at for at in range(ways.bit_length() - 1)]
    steps = len(bits)
    me = lax.axis_index("ctx")
    core = lax.axis_index("seq")

    def other(bit):
        return me + bit - 2 * bit * ((me // bit) % 2)

    barrier = pltpu.get_barrier_semaphore()
    for bit in bits:
        pl.semaphore_signal(barrier, inc=1, device_id={"ctx": other(bit)}, device_id_type=MESH)
    pl.semaphore_signal(barrier, inc=1, device_id={"seq": 1 - core}, device_id_type=MESH)
    pl.semaphore_wait(barrier, steps + 1)

    def place(which, unit):
        across = sizes[which][1] // unit_cols
        row = pl.multiple_of((unit // across) * unit_rows, unit_rows)
        col = pl.multiple_of((unit % across) * unit_cols, unit_cols)
        return row, col

    def each(work, share=0, shares=1):
        base = 0
        for which, (rows, cols) in enumerate(sizes):
            units = (rows // unit_rows) * (cols // unit_cols)

            def pair(at, carry, which=which, base=base):
                for turn in range(2):
                    unit = 2 * at + turn
                    row, col = place(which, unit)
                    work(which, base + unit, turn, row, col)
                return carry

            pairs = units // 2
            lax.fori_loop(pairs * share // shares, pairs * (share + 1) // shares, pair, 0)
            base += units

    def order(turn):
        return [bits[1], bits[0]] + bits[2:] if turn else bits

    def cuts(turn):
        first, length, found = 0, unit_rows, []
        for bit in order(turn):
            length //= 2
            mine = (me // bit) % 2
            found.append((first + mine * length, first + (1 - mine) * length, length))
            first = first + mine * length
        return found

    def rows_of(first, length):
        return pl.ds(pl.multiple_of(first, UNIT_ROWS), length)

    def here(which, unit, row, col):
        start = pl.multiple_of(core * sizes[which][0] + row, unit_rows)
        return pltpu.make_async_copy(
            parts[which].at[pl.ds(start, unit_rows), pl.ds(col, unit_cols)],
            own.at[unit],
            here_sem.at[unit],
        )

    def across(which, unit, row, col):
        start = pl.multiple_of((1 - core) * sizes[which][0] + row, unit_rows)
        return pltpu.make_async_remote_copy(
            src_ref=parts[which].at[pl.ds(start, unit_rows), pl.ds(col, unit_cols)],
            dst_ref=far.at[unit],
            send_sem=far_send.at[unit],
            recv_sem=far_recv.at[unit],
            device_id={"seq": 1 - core},
            device_id_type=MESH,
        )

    def scatter(step, unit, turn):
        stays, goes, length = cuts(turn)[step]
        if step == 0:
            source = own.at[unit, rows_of(goes, length)]
        else:
            kept_first = cuts(turn)[0][0]
            source = kept.at[unit, rows_of(goes - kept_first, length)]
        return pltpu.make_async_remote_copy(
            src_ref=source,
            dst_ref=near.at[unit, pl.ds(unit_rows - 2 * length, length)],
            send_sem=send.at[step, unit],
            recv_sem=recv.at[step, unit],
            device_id={"ctx": other(order(turn)[step])},
            device_id_type=MESH,
        )

    def gather(step, which, unit, turn, row, col):
        stays, goes, length = cuts(turn)[step]
        held = outs[which].at[rows_of(row + stays, length), pl.ds(col, unit_cols)]
        return pltpu.make_async_remote_copy(
            src_ref=held,
            dst_ref=held,
            send_sem=back_send.at[step, unit],
            recv_sem=back_recv.at[step, unit],
            device_id={"ctx": other(order(turn)[step])},
            device_id_type=MESH,
        )

    def add(left, right):
        return (left.astype(jnp.float32) + right.astype(jnp.float32)).astype(jnp.bfloat16)

    def launch(which, unit, turn, row, col):
        here(which, unit, row, col).start()
        across(which, unit, row, col).start()

    def first(which, unit, turn, row, col):
        here(which, unit, row, col).wait()
        across(which, unit, row, col).wait_recv()
        own[unit] = add(own[unit], far[unit])
        scatter(0, unit, turn).start()

    def middle(step, which, unit, turn, row, col):
        scatter(step, unit, turn).wait_recv()
        stays, goes, length = cuts(turn)[step]
        arrived = near[unit, pl.ds(unit_rows - 2 * length, length)]
        if step == 0:
            total = add(own[unit, rows_of(stays, length)], arrived)
        else:
            total = add(kept[unit, rows_of(stays - cuts(turn)[0][0], length)], arrived)
        if step < steps - 1:
            kept[unit, rows_of(stays - cuts(turn)[0][0], length)] = total
            scatter(step + 1, unit, turn).start()
        else:
            outs[which][rows_of(row + stays, length), pl.ds(col, unit_cols)] = total
            gather(step, which, unit, turn, row, col).start()

    def spread(step, which, unit, turn, row, col):
        gather(step, which, unit, turn, row, col).wait_recv()
        if step > 0:
            gather(step - 1, which, unit, turn, row, col).start()

    def finish(which, unit, turn, row, col):
        across(which, unit, row, col).wait_send()
        for step in range(steps):
            scatter(step, unit, turn).wait_send()
            gather(step, which, unit, turn, row, col).wait_send()

    stages = [launch, first]
    stages += [functools.partial(middle, step) for step in range(steps)]
    stages += [functools.partial(spread, step) for step in reversed(range(steps))]
    stages += [finish]
    return [functools.partial(each, stage) for stage in stages]


def sum_kernel(sizes, ways, unit_cols, *refs):
    for stage in sum_plan(sizes, ways, unit_cols, refs):
        stage()


def sum_attend_kernel(sizes, ways, unit_cols, rows, *refs):
    count = len(sizes)
    query_ref, query_t_ref, key_ref, key_t_ref, value_ref, grad_ref, grad_t_ref = refs[:7]
    log_ref, delta_ref = refs[7:9]
    parts = refs[9 : 9 + count]
    query_grad_ref, key_grad_ref, value_grad_ref = refs[9 + count : 12 + count]
    outs = refs[12 + count : 12 + 2 * count]
    query_acc = refs[12 + 2 * count]
    stages = sum_plan(sizes, ways, unit_cols, (*parts, *outs, *refs[13 + 2 * count :]))
    stages[0]()
    shares = 4
    tasks = [stages[1]]
    tasks += [functools.partial(stage, share, shares) for stage in stages[2:-1] for share in range(shares)]
    tasks += [stages[-1]]
    blocks = query_t_ref.shape[1] // rows
    query_acc[...] = jnp.zeros_like(query_acc)

    def column(at, carry):
        start = pl.multiple_of(at * rows, rows)
        own = pl.ds(start, rows)

        def advance(block, kept, masked):
            key_sum, value_sum = kept
            first = pl.multiple_of(block * rows, rows)
            part = pl.ds(first, rows)
            scores = dot(key_ref[own, :], query_t_ref[:, part])
            probs = jnp.exp(scores - log_ref[:, part])
            if masked:
                probs = jnp.where(diagonal(rows), probs, 0.0)
            prob_grad = dot(value_ref[own, :], grad_t_ref[:, part])
            score_grad = (probs * (prob_grad - delta_ref[:, part])).astype(jnp.bfloat16)
            value_sum = value_sum + dot(probs.astype(jnp.bfloat16), grad_ref[part, :])
            key_sum = key_sum + dot(score_grad, query_ref[part, :])
            query_acc[:, part] += dot(key_t_ref[:, own], score_grad)
            return key_sum, value_sum

        zero = jnp.zeros((rows, HEAD_DIM), jnp.float32)
        state = advance(at, (zero, zero), True)
        key_sum, value_sum = lax.fori_loop(
            at + 1, blocks, lambda block, kept: advance(block, kept, False), state
        )
        key_grad_ref[own, :] = key_sum.astype(jnp.bfloat16)
        value_grad_ref[own, :] = value_sum.astype(jnp.bfloat16)
        for turn, task in enumerate(tasks[:blocks]):
            pl.when(at == turn)(task)
        return carry

    lax.fori_loop(0, blocks, column, 0)
    query_grad_ref[...] = (query_acc[...] * HEAD_DIM**-0.5).astype(jnp.bfloat16)
    for task in tasks[blocks:]:
        task()


def unit_columns(parts):
    return math.gcd(1024, *[part.shape[1] for part in parts])


def can_sum(parts):
    ways, cores = lax.axis_size("ctx"), lax.axis_size("seq")
    if cores != 2 or ways < 4 or ways & (ways - 1):
        return False
    for part in parts:
        rows = part.shape[0] // cores
        units = rows // (UNIT_ROWS * ways) * (part.shape[1] // unit_columns(parts))
        if rows % (UNIT_ROWS * ways) or units % 2:
            return False
    return True


def sum_scratch(sizes, ways, unit_cols):
    unit = (UNIT_ROWS * ways, unit_cols)
    units = sum(rows * cols for rows, cols in sizes) // (unit[0] * unit[1])
    steps = ways.bit_length() - 1
    bf16, dma = jnp.bfloat16, pltpu.SemaphoreType.DMA
    return [
        pltpu.VMEM((units, *unit), bf16),
        pltpu.VMEM((units, *unit), bf16),
        pltpu.VMEM((units, *unit), bf16),
        pltpu.VMEM((units, unit[0] // 2, unit[1]), bf16),
        dma((units,)),
        dma((units,)),
        dma((units,)),
        dma((steps, units)),
        dma((steps, units)),
        dma((steps, units)),
        dma((steps, units)),
    ]


def total_grads(call, parts):
    if not can_sum(parts):
        return [total_grad(part) for part in parts]
    ways = lax.axis_size("ctx")
    unit_cols = unit_columns(parts)
    sizes = [(part.shape[0] // 2, part.shape[1]) for part in parts]
    sums = pl.pallas_call(
        functools.partial(sum_kernel, sizes, ways, unit_cols),
        in_specs=[pl.BlockSpec(memory_space=pl.ANY)] * len(parts),
        out_specs=[pl.BlockSpec(memory_space=pltpu.VMEM)] * len(parts),
        out_shape=[jax.ShapeDtypeStruct(size, jnp.bfloat16) for size in sizes],
        scratch_shapes=sum_scratch(sizes, ways, unit_cols),
        compiler_params=pltpu.CompilerParams(
            collective_id=call, has_side_effects=True, vmem_limit_bytes=56 * 2**20
        ),
    )(*[part.astype(jnp.bfloat16) for part in parts])
    return [item.astype(jnp.float32) for item in sums]


def attend_back_sum(call, operands, parts, rows):
    ways = lax.axis_size("ctx")
    unit_cols = unit_columns(parts)
    sizes = [(part.shape[0] // 2, part.shape[1]) for part in parts]
    operands = [item[0] for item in operands]
    length, features = operands[0].shape
    bf16 = jnp.bfloat16
    vmem = pl.BlockSpec(memory_space=pltpu.VMEM)
    query_grad, key_grad, value_grad, *sums = pl.pallas_call(
        functools.partial(sum_attend_kernel, sizes, ways, unit_cols, rows),
        in_specs=[vmem] * len(operands) + [pl.BlockSpec(memory_space=pl.ANY)] * len(parts),
        out_specs=[vmem] * (3 + len(parts)),
        out_shape=[
            jax.ShapeDtypeStruct((features, length), bf16),
            jax.ShapeDtypeStruct((length, features), bf16),
            jax.ShapeDtypeStruct((length, features), bf16),
            *[jax.ShapeDtypeStruct(size, bf16) for size in sizes],
        ],
        scratch_shapes=[
            pltpu.VMEM((features, length), jnp.float32),
            *sum_scratch(sizes, ways, unit_cols),
        ],
        compiler_params=pltpu.CompilerParams(
            collective_id=call, has_side_effects=True, vmem_limit_bytes=60 * 2**20
        ),
    )(*operands, *[part.astype(bf16) for part in parts])
    grads = [query_grad[None], key_grad.T[None], value_grad.T[None]]
    return grads, [item.astype(jnp.float32) for item in sums]


def local(
    layer_input,
    ln1_gain,
    ln1_bias,
    qkv_weight,
    query_bias,
    value_bias,
    out_weight,
    out_bias,
    ln2_gain,
    ln2_bias,
    up_weight,
    up_bias,
    down_weight,
    down_bias,
    out_cotangent,
):
    small = (
        ln1_gain,
        ln1_bias,
        query_bias,
        value_bias,
        out_bias,
        ln2_gain,
        ln2_bias,
        up_bias,
        down_bias,
    )
    sizes = [item.shape[0] for item in small]
    cuts = [sum(sizes[: at + 1]) for at in range(len(sizes) - 1)]
    small_full = lax.all_gather(jnp.concatenate(small), "seq", axis=0)
    (gain_one, shift_one, q_bias, v_bias, o_bias, gain_two, shift_two, u_bias, d_bias) = [
        item.reshape(-1) for item in jnp.split(small_full, cuts, axis=1)
    ]
    qkv_full = lax.all_gather(qkv_weight, "seq", axis=0, tiled=True)
    out_full = lax.all_gather(out_weight, "seq", axis=0, tiled=True)
    up_full = lax.all_gather(up_weight, "seq", axis=0, tiled=True)
    down_full = lax.all_gather(down_weight, "seq", axis=0, tiled=True)
    seq_count, block_len, model_width = layer_input.shape
    f32 = jnp.float32
    bf16 = jnp.bfloat16
    input_f32 = layer_input.astype(f32)
    gain_one_f = gain_one.astype(f32)
    shift_one_f = shift_one.astype(f32)
    gain_two_f = gain_two.astype(f32)
    shift_two_f = shift_two.astype(f32)
    normed_one = layer_norm(input_f32, gain_one_f, shift_one_f).astype(bf16)
    projected = jnp.einsum("std,de->ste", normed_one, qkv_full, preferred_element_type=f32)
    queries = (projected[..., :model_width] + q_bias.astype(f32)).astype(bf16)
    keys = projected[..., model_width : 2 * model_width].astype(bf16)
    values = (projected[..., 2 * model_width :] + v_bias.astype(f32)).astype(bf16)
    by_heads = HEADS % lax.axis_size("ctx") == 0
    if by_heads:
        attention_low, kept_heads = head_forward(queries, keys, values)
    else:
        attention, log_total = block_forward(queries, keys, values)
        attention_low = attention.astype(bf16)
    mid = (
        input_f32
        + jnp.einsum("std,de->ste", attention_low, out_full, preferred_element_type=f32)
        + o_bias.astype(f32)
    )
    normed_two = layer_norm(mid, gain_two_f, shift_two_f).astype(bf16)
    hidden = jnp.einsum(
        "std,df->stf", normed_two, up_full, preferred_element_type=f32
    ) + u_bias.astype(f32)
    activated = jax.nn.gelu(hidden).astype(bf16)
    result = (
        mid
        + jnp.einsum("stf,fd->std", activated, down_full, preferred_element_type=f32)
        + d_bias.astype(f32)
    )
    layer_output = result.astype(bf16)
    cotangent_f = out_cotangent.astype(f32)
    down_bias_grad = jnp.sum(cotangent_f, axis=(0, 1))
    down_weight_grad = jnp.einsum(
        "stf,std->fd", activated, out_cotangent, preferred_element_type=f32
    )
    act_grad = jnp.einsum("std,fd->stf", out_cotangent, down_full, preferred_element_type=f32)
    unused_gelu, gelu_pull = jax.vjp(jax.nn.gelu, hidden)
    hidden_grad = gelu_pull(act_grad)[0].astype(bf16)
    up_bias_grad = jnp.sum(hidden_grad.astype(f32), axis=(0, 1))
    up_weight_grad = jnp.einsum("std,stf->df", normed_two, hidden_grad, preferred_element_type=f32)
    normed_two_grad = jnp.einsum("stf,df->std", hidden_grad, up_full, preferred_element_type=f32)
    unused_two, norm_two_pull = jax.vjp(layer_norm, mid, gain_two_f, shift_two_f)
    mid_norm_grad, ln2_gain_grad, ln2_bias_grad = norm_two_pull(normed_two_grad)
    mid_grad = cotangent_f + mid_norm_grad
    branch_grad = mid_grad.astype(bf16)
    out_bias_grad = jnp.sum(branch_grad.astype(f32), axis=(0, 1))
    out_weight_grad = jnp.einsum(
        "std,ste->de", attention_low, branch_grad, preferred_element_type=f32
    )
    attention_grad = jnp.einsum(
        "ste,de->std", branch_grad, out_full, preferred_element_type=f32
    ).astype(bf16)
    if by_heads:
        (query_low, key_low, value_low), (up_sum, down_sum) = head_backward(
            kept_heads, attention_grad, [up_weight_grad, down_weight_grad]
        )
    else:
        query_low, key_low, value_low = block_backward(
            queries, keys, values, attention, log_total, attention_grad
        )
        up_sum, down_sum = total_grads(0, [up_weight_grad, down_weight_grad])
    query_bias_grad = jnp.sum(query_low.astype(f32), axis=(0, 1))
    value_bias_grad = jnp.sum(value_low.astype(f32), axis=(0, 1))
    joined_grad = jnp.concatenate([query_low, key_low, value_low], axis=-1)
    qkv_weight_grad = jnp.einsum("std,ste->de", normed_one, joined_grad, preferred_element_type=f32)
    normed_one_grad = jnp.einsum("ste,de->std", joined_grad, qkv_full, preferred_element_type=f32)
    unused_one, norm_one_pull = jax.vjp(layer_norm, input_f32, gain_one_f, shift_one_f)
    input_norm_grad, ln1_gain_grad, ln1_bias_grad = norm_one_pull(normed_one_grad)
    input_grad = mid_grad + input_norm_grad
    small_grads = (
        ln1_gain_grad,
        ln1_bias_grad,
        query_bias_grad,
        value_bias_grad,
        out_bias_grad,
        ln2_gain_grad,
        ln2_bias_grad,
        up_bias_grad,
        down_bias_grad,
    )
    ways = lax.axis_size("seq")
    small_sum = total_grad(
        jnp.concatenate([item.reshape(ways, -1) for item in small_grads], axis=1)
    )[0]
    (
        ln1_gain_sum,
        ln1_bias_sum,
        query_bias_sum,
        value_bias_sum,
        out_bias_sum,
        ln2_gain_sum,
        ln2_bias_sum,
        up_bias_sum,
        down_bias_sum,
    ) = jnp.split(small_sum, cuts)
    qkv_sum, out_sum = total_grads(1, [qkv_weight_grad, out_weight_grad])
    return (
        layer_output,
        input_grad,
        ln1_gain_sum,
        ln1_bias_sum,
        qkv_sum,
        query_bias_sum,
        value_bias_sum,
        out_sum,
        out_bias_sum,
        ln2_gain_sum,
        ln2_bias_sum,
        up_sum,
        up_bias_sum,
        down_sum,
        down_bias_sum,
    )


def solution(mesh):
    return jax.shard_map(
        local,
        mesh=mesh,
        in_specs=(
            P("seq", "ctx", None),
            P("seq"),
            P("seq"),
            P("seq", None),
            P("seq"),
            P("seq"),
            P("seq", None),
            P("seq"),
            P("seq"),
            P("seq"),
            P("seq", None),
            P("seq"),
            P("seq", None),
            P("seq"),
            P("seq", "ctx", None),
        ),
        out_specs=(
            P("seq", "ctx", None),
            P("seq", "ctx", None),
            P("seq"),
            P("seq"),
            P("seq", None),
            P("seq"),
            P("seq"),
            P("seq", None),
            P("seq"),
            P("seq"),
            P("seq"),
            P("seq", None),
            P("seq"),
            P("seq", None),
            P("seq"),
        ),
        check_vma=False,
    )
```

```python
import functools
import math

import jax
import jax.numpy as jnp
from jax import lax
from jax.experimental import pallas as pl
from jax.experimental.pallas import tpu as pltpu
from jax.sharding import PartitionSpec as P

HEADS = 16
HEAD_DIM = 64


EPS = 1e-05
FLOOR_SCORE = -1e30
UNIT_ROWS = 16


def layer_norm(values, gain, shift):
    centre = values - jnp.mean(values, axis=-1, keepdims=True)
    spread = jnp.mean(centre * centre, axis=-1, keepdims=True)
    return centre * lax.rsqrt(spread + EPS) * gain + shift


def split_heads(values):
    return values.reshape(values.shape[0], values.shape[1], HEADS, HEAD_DIM)


def causal(query_first, query_rows, key_first, key_rows):
    query_pos = query_first + jnp.arange(query_rows, dtype=jnp.int32)
    key_pos = key_first + jnp.arange(key_rows, dtype=jnp.int32)
    return key_pos[None, :] <= query_pos[:, None]


def over_blocks(running, arrays, advance):
    piece_rows = arrays[0].shape[1]
    block_rows = math.gcd(piece_rows, 512)
    pieces = piece_rows // block_rows
    stacked = tuple(
        (
            jnp.moveaxis(item.reshape(item.shape[:1] + (pieces, block_rows) + item.shape[2:]), 1, 0)
            for item in arrays
        )
    )

    def inner(kept, pair):
        blocks, position = pair
        return (advance(kept, blocks, position * block_rows), None)

    result, unused = lax.scan(inner, running, (stacked, jnp.arange(pieces, dtype=jnp.int32)))
    return result


def dot(left, right, left_axis=1, right_axis=0):
    return lax.dot_general(
        left, right, (((left_axis,), (right_axis,)), ((), ())), preferred_element_type=jnp.float32
    )


def diagonal(rows):
    key_at = lax.broadcasted_iota(jnp.int32, (rows, rows), 0)
    query_at = lax.broadcasted_iota(jnp.int32, (rows, rows), 1)
    return key_at <= query_at


def forward_kernel(rows, query_ref, key_ref, value_ref, out_ref, log_ref):
    at = pl.program_id(1)
    query = query_ref[0]

    def advance(block, kept, masked):
        top, total, accum = kept
        first = pl.multiple_of(block * rows, rows)
        scores = dot(key_ref[0, pl.ds(first, rows), :], query)
        if masked:
            scores = jnp.where(diagonal(rows), scores, FLOOR_SCORE)
        new_top = jnp.maximum(top, jnp.max(scores, axis=0, keepdims=True))
        weights = jnp.exp(scores - new_top)
        factor = jnp.exp(top - new_top)
        total = total * factor + jnp.sum(weights, axis=0, keepdims=True)
        mixed = dot(value_ref[0, :, pl.ds(first, rows)], weights.astype(jnp.bfloat16))
        return new_top, total, accum * factor + mixed

    state = (
        jnp.full((1, rows), FLOOR_SCORE, jnp.float32),
        jnp.zeros((1, rows), jnp.float32),
        jnp.zeros((HEAD_DIM, rows), jnp.float32),
    )
    state = lax.fori_loop(0, at, lambda block, kept: advance(block, kept, False), state)
    top, total, accum = advance(at, state, True)
    out_ref[0] = accum / total
    log_ref[0] = top + jnp.log(total)


def attend(query_t, key, value_t, rows):
    batch, features, length = query_t.shape
    pairs = batch * length * (length + rows) // 2
    return pl.pallas_call(
        functools.partial(forward_kernel, rows),
        grid=(batch, length // rows),
        in_specs=[
            pl.BlockSpec((1, features, rows), lambda b, i: (b, 0, i)),
            pl.BlockSpec((1, length, features), lambda b, i: (b, 0, 0)),
            pl.BlockSpec((1, features, length), lambda b, i: (b, 0, 0)),
        ],
        out_specs=[
            pl.BlockSpec((1, features, rows), lambda b, i: (b, 0, i)),
            pl.BlockSpec((1, 1, rows), lambda b, i: (b, 0, i)),
        ],
        out_shape=[
            jax.ShapeDtypeStruct((batch, features, length), jnp.float32),
            jax.ShapeDtypeStruct((batch, 1, length), jnp.float32),
        ],
        compiler_params=pltpu.CompilerParams(vmem_limit_bytes=48 * 2**20),
        cost_estimate=pl.CostEstimate(
            flops=4 * features * pairs, bytes_accessed=16 * features * length, transcendentals=pairs
        ),
    )(query_t, key, value_t)


def backward_kernel(
    rows,
    query_ref,
    query_t_ref,
    key_ref,
    key_t_ref,
    value_ref,
    grad_ref,
    grad_t_ref,
    log_ref,
    delta_ref,
    query_grad_ref,
    key_grad_ref,
    value_grad_ref,
    query_acc,
):
    at = pl.program_id(1)
    blocks = pl.num_programs(1)
    key = key_ref[0]
    key_t = key_t_ref[0]
    value = value_ref[0]

    @pl.when(at == 0)
    def clear():
        query_acc[...] = jnp.zeros_like(query_acc)

    def advance(block, kept, masked):
        key_sum, value_sum = kept
        first = pl.multiple_of(block * rows, rows)
        part = pl.ds(first, rows)
        scores = dot(key, query_t_ref[0, :, part])
        probs = jnp.exp(scores - log_ref[0, :, part])
        if masked:
            probs = jnp.where(diagonal(rows), probs, 0.0)
        prob_grad = dot(value, grad_t_ref[0, :, part])
        score_grad = (probs * (prob_grad - delta_ref[0, :, part])).astype(jnp.bfloat16)
        value_sum = value_sum + dot(probs.astype(jnp.bfloat16), grad_ref[0, part, :])
        key_sum = key_sum + dot(score_grad, query_ref[0, part, :])
        query_acc[:, part] += dot(key_t, score_grad)
        return key_sum, value_sum

    zero = jnp.zeros((rows, HEAD_DIM), jnp.float32)
    state = advance(at, (zero, zero), True)
    key_sum, value_sum = lax.fori_loop(
        at + 1, blocks, lambda block, kept: advance(block, kept, False), state
    )
    key_grad_ref[0] = key_sum.T.astype(jnp.bfloat16)
    value_grad_ref[0] = value_sum.T.astype(jnp.bfloat16)

    @pl.when(at == blocks - 1)
    def finish():
        query_grad_ref[0] = (query_acc[...] * HEAD_DIM**-0.5).astype(jnp.bfloat16)


def attend_back(query, query_t, key, key_t, value, grad, grad_t, log_total, delta, rows):
    batch, features, length = query_t.shape
    pairs = batch * length * (length + rows) // 2
    whole = pl.BlockSpec((1, length, features), lambda b, j: (b, 0, 0))
    whole_t = pl.BlockSpec((1, features, length), lambda b, j: (b, 0, 0))
    piece = pl.BlockSpec((1, rows, features), lambda b, j: (b, j, 0))
    piece_t = pl.BlockSpec((1, features, rows), lambda b, j: (b, 0, j))
    line = pl.BlockSpec((1, 1, length), lambda b, j: (b, 0, 0))
    shape = jax.ShapeDtypeStruct((batch, features, length), jnp.bfloat16)
    return pl.pallas_call(
        functools.partial(backward_kernel, rows),
        grid=(batch, length // rows),
        in_specs=[whole, whole_t, piece, piece_t, piece, whole, whole_t, line, line],
        out_specs=[whole_t, piece_t, piece_t],
        out_shape=[shape, shape, shape],
        scratch_shapes=[pltpu.VMEM((features, length), jnp.float32)],
        compiler_params=pltpu.CompilerParams(vmem_limit_bytes=48 * 2**20),
        cost_estimate=pl.CostEstimate(
            flops=10 * features * pairs, bytes_accessed=24 * features * length, transcendentals=pairs
        ),
    )(query, query_t, key, key_t, value, grad, grad_t, log_total, delta)


def to_heads(values_t, ways):
    seqs, parts, width, rows = values_t.shape
    own = HEADS // ways
    cut = values_t.reshape(seqs, parts, ways, own, HEAD_DIM, rows)
    cut = jnp.transpose(cut, (2, 1, 0, 3, 4, 5))
    moved = lax.all_to_all(cut, "ctx", 0, 0)
    joined = jnp.transpose(moved, (1, 2, 3, 4, 0, 5))
    return joined.reshape(parts, seqs * own, HEAD_DIM, ways * rows)


def to_positions(values_t, ways, seqs):
    parts, batch, features, length = values_t.shape
    own = HEADS // ways
    cut = values_t.reshape(parts, seqs, own, features, ways, length // ways)
    cut = jnp.transpose(cut, (4, 0, 1, 2, 3, 5))
    moved = lax.all_to_all(cut, "ctx", 0, 0)
    joined = jnp.transpose(moved, (2, 1, 0, 3, 4, 5))
    return joined.reshape(seqs, parts, HEADS * HEAD_DIM, length // ways)


def head_forward(queries, keys, values):
    ways = lax.axis_size("ctx")
    scale = jnp.asarray(HEAD_DIM**-0.5, jnp.bfloat16)
    stacked = jnp.stack([queries * scale, keys, values], axis=1)
    query_t, key_t, value_t = to_heads(jnp.swapaxes(stacked, 2, 3), ways)
    rows = math.gcd(query_t.shape[2], 512)
    key = jnp.swapaxes(key_t, 1, 2)
    out_t, log_total = attend(query_t, key, value_t, rows)
    low_t = to_positions(out_t[None].astype(jnp.bfloat16), ways, queries.shape[0])[:, 0]
    return jnp.swapaxes(low_t, 1, 2), (query_t, key, key_t, value_t, out_t, log_total)


def head_backward(kept, attention_grad, parts):
    query_t, key, key_t, value_t, out_t, log_total = kept
    ways = lax.axis_size("ctx")
    seqs = attention_grad.shape[0]
    (grad_t,) = to_heads(jnp.swapaxes(attention_grad, 1, 2)[:, None], ways)
    delta = jnp.sum(grad_t.astype(jnp.float32) * out_t, axis=1, keepdims=True)
    operands = (
        jnp.swapaxes(query_t, 1, 2),
        query_t,
        key,
        key_t,
        jnp.swapaxes(value_t, 1, 2),
        jnp.swapaxes(grad_t, 1, 2),
        grad_t,
        log_total,
        delta,
    )
    rows = math.gcd(query_t.shape[2], 512)
    if query_t.shape[0] == 1 and can_sum(parts):
        grads, sums = attend_back_sum(0, operands, parts, rows)
    else:
        grads = attend_back(*operands, rows)
        sums = total_grads(0, parts)
    back = to_positions(jnp.stack(grads), ways, seqs)
    return [jnp.swapaxes(back[:, at], 1, 2) for at in range(3)], sums


def block_forward(queries, keys, values):
    seq_count, block_len, model_width = queries.shape
    scale_factor = HEAD_DIM ** (-0.5)
    my_start = lax.axis_index("ctx") * block_len
    f32 = jnp.float32
    bf16 = jnp.bfloat16
    query_heads = split_heads(queries)

    def forward_block(running, blocks, key_start):
        key_block, value_block = blocks
        key_rows = key_block.shape[1]

        def forward_compute(kept):
            top, total, accum = kept
            allowed = causal(my_start, block_len, key_start, key_rows)
            scores = (
                jnp.einsum(
                    "sqhd,skhd->shqk",
                    query_heads,
                    split_heads(key_block),
                    preferred_element_type=f32,
                )
                * scale_factor
            )
            scores = jnp.where(allowed, scores, FLOOR_SCORE)
            new_top = jnp.maximum(top, jnp.max(scores, axis=-1))
            factor = jnp.exp(top - new_top)
            weights = jnp.where(allowed, jnp.exp(scores - new_top[..., None]), 0.0)
            new_total = total * factor + jnp.sum(weights, axis=-1)
            mixed = jnp.einsum(
                "shqk,skhd->sqhd",
                weights.astype(bf16),
                split_heads(value_block),
                preferred_element_type=f32,
            )
            new_accum = accum * jnp.transpose(factor, (0, 2, 1))[..., None] + mixed
            return (new_top, new_total, new_accum)

        return lax.cond(
            key_start > my_start + block_len - 1, lambda kept: kept, forward_compute, running
        )

    start_state = (
        jnp.full((seq_count, HEADS, block_len), FLOOR_SCORE, f32),
        jnp.zeros((seq_count, HEADS, block_len), f32),
        jnp.zeros((seq_count, block_len, HEADS, HEAD_DIM), f32),
    )
    top, total, accum = over_blocks(
        start_state,
        (
            lax.all_gather(keys, "ctx", axis=1, tiled=True),
            lax.all_gather(values, "ctx", axis=1, tiled=True),
        ),
        forward_block,
    )
    attention = (accum / jnp.transpose(total, (0, 2, 1))[..., None]).reshape(
        seq_count, block_len, model_width
    )
    log_total = top + jnp.log(total)
    return attention, log_total


def block_backward(queries, keys, values, attention, log_total, attention_grad):
    seq_count, block_len, model_width = queries.shape
    scale_factor = HEAD_DIM ** (-0.5)
    my_start = lax.axis_index("ctx") * block_len
    f32 = jnp.float32
    bf16 = jnp.bfloat16
    query_heads = split_heads(queries)

    grad_heads = split_heads(attention_grad)
    delta_rows = jnp.sum(split_heads(attention_grad.astype(f32) * attention), axis=-1)
    delta_heads = jnp.transpose(delta_rows, (0, 2, 1))

    def keys_block(running, blocks, key_start):
        key_block, value_block = blocks
        key_rows = key_block.shape[1]

        def keys_compute(kept):
            query_acc, key_grads, value_grads = kept
            allowed = causal(my_start, block_len, key_start, key_rows)
            block_keys = split_heads(key_block)
            scores = (
                jnp.einsum("sqhd,skhd->shqk", query_heads, block_keys, preferred_element_type=f32)
                * scale_factor
            )
            probs = jnp.where(allowed, jnp.exp(scores - log_total[..., None]), 0.0)
            prob_grad = jnp.einsum(
                "sqhd,skhd->shqk", grad_heads, split_heads(value_block), preferred_element_type=f32
            )
            score_grad = (probs * (prob_grad - delta_heads[..., None])).astype(bf16)
            query_acc = (
                query_acc
                + jnp.einsum("shqk,skhd->sqhd", score_grad, block_keys, preferred_element_type=f32)
                * scale_factor
            )
            key_term = (
                jnp.einsum("shqk,sqhd->skhd", score_grad, query_heads, preferred_element_type=f32)
                * scale_factor
            ).reshape(seq_count, key_rows, model_width)
            value_term = jnp.einsum(
                "shqk,sqhd->skhd", probs.astype(bf16), grad_heads, preferred_element_type=f32
            ).reshape(seq_count, key_rows, model_width)
            key_grads = lax.dynamic_update_slice_in_dim(key_grads, key_term, key_start, 1)
            value_grads = lax.dynamic_update_slice_in_dim(value_grads, value_term, key_start, 1)
            return (query_acc, key_grads, value_grads)

        return lax.cond(
            key_start > my_start + block_len - 1, lambda kept: kept, keys_compute, running
        )

    whole_len = block_len * lax.axis_size("ctx")
    keys_state = (
        jnp.zeros((seq_count, block_len, HEADS, HEAD_DIM), f32),
        jnp.zeros((seq_count, whole_len, model_width), f32),
        jnp.zeros((seq_count, whole_len, model_width), f32),
    )
    query_acc, key_grads, value_grads = over_blocks(
        keys_state,
        (
            lax.all_gather(keys, "ctx", axis=1, tiled=True),
            lax.all_gather(values, "ctx", axis=1, tiled=True),
        ),
        keys_block,
    )
    query_sum = query_acc.reshape(seq_count, block_len, model_width)
    key_sum, value_sum = (
        lax.psum_scatter(
            key_grads.astype(jnp.bfloat16), "ctx", scatter_dimension=1, tiled=True
        ).astype(jnp.float32),
        lax.psum_scatter(
            value_grads.astype(jnp.bfloat16), "ctx", scatter_dimension=1, tiled=True
        ).astype(jnp.float32),
    )
    return query_sum.astype(bf16), key_sum.astype(bf16), value_sum.astype(bf16)


def total_grad(part):
    owned = lax.psum_scatter(part.astype(jnp.bfloat16), "seq", scatter_dimension=0, tiled=True)
    return lax.psum(owned, "ctx").astype(jnp.float32)


MESH = pl.DeviceIdType.MESH


def sum_plan(sizes, ways, unit_cols, refs):
    count = len(sizes)
    parts, outs = refs[:count], refs[count : 2 * count]
    own, far, near, kept, here_sem, far_send, far_recv, send, recv, back_send, back_recv = refs[
        2 * count :
    ]
    unit_rows = UNIT_ROWS * ways
    bits = [2**at for at in range(ways.bit_length() - 1)]
    steps = len(bits)
    me = lax.axis_index("ctx")
    core = lax.axis_index("seq")

    def other(bit):
        return me + bit - 2 * bit * ((me // bit) % 2)

    barrier = pltpu.get_barrier_semaphore()
    for bit in bits:
        pl.semaphore_signal(barrier, inc=1, device_id={"ctx": other(bit)}, device_id_type=MESH)
    pl.semaphore_signal(barrier, inc=1, device_id={"seq": 1 - core}, device_id_type=MESH)
    pl.semaphore_wait(barrier, steps + 1)

    def place(which, unit):
        across = sizes[which][1] // unit_cols
        row = pl.multiple_of((unit // across) * unit_rows, unit_rows)
        col = pl.multiple_of((unit % across) * unit_cols, unit_cols)
        return row, col

    def each(work, share=0, shares=1):
        base = 0
        for which, (rows, cols) in enumerate(sizes):
            units = (rows // unit_rows) * (cols // unit_cols)

            def one(unit, carry, turn=0, which=which, base=base):
                row, col = place(which, unit)
                work(which, base + unit, turn, row, col)
                return carry

            def pair(at, carry, one=one):
                return one(2 * at + 1, one(2 * at, carry), 1)

            pairs = units // 2
            lax.fori_loop(pairs * share // shares, pairs * (share + 1) // shares, pair, 0)
            if units % 2 and share == shares - 1:
                lax.fori_loop(units - 1, units, one, 0)
            base += units

    def order(turn):
        return [bits[1], bits[0]] + bits[2:] if turn else bits

    def cuts(turn):
        first, length, found = 0, unit_rows, []
        for bit in order(turn):
            length //= 2
            mine = (me // bit) % 2
            found.append((first + mine * length, first + (1 - mine) * length, length))
            first = first + mine * length
        return found

    def rows_of(first, length):
        return pl.ds(pl.multiple_of(first, UNIT_ROWS), length)

    def here(which, unit, row, col):
        start = pl.multiple_of(core * sizes[which][0] + row, unit_rows)
        return pltpu.make_async_copy(
            parts[which].at[pl.ds(start, unit_rows), pl.ds(col, unit_cols)],
            own.at[unit],
            here_sem.at[unit],
        )

    def across(which, unit, row, col):
        start = pl.multiple_of((1 - core) * sizes[which][0] + row, unit_rows)
        return pltpu.make_async_remote_copy(
            src_ref=parts[which].at[pl.ds(start, unit_rows), pl.ds(col, unit_cols)],
            dst_ref=far.at[unit],
            send_sem=far_send.at[unit],
            recv_sem=far_recv.at[unit],
            device_id={"seq": 1 - core},
            device_id_type=MESH,
        )

    def scatter(step, unit, turn):
        stays, goes, length = cuts(turn)[step]
        if step == 0:
            source = own.at[unit, rows_of(goes, length)]
        else:
            kept_first = cuts(turn)[0][0]
            source = kept.at[unit, rows_of(goes - kept_first, length)]
        return pltpu.make_async_remote_copy(
            src_ref=source,
            dst_ref=near.at[unit, pl.ds(unit_rows - 2 * length, length)],
            send_sem=send.at[step, unit],
            recv_sem=recv.at[step, unit],
            device_id={"ctx": other(order(turn)[step])},
            device_id_type=MESH,
        )

    def gather(step, which, unit, turn, row, col):
        stays, goes, length = cuts(turn)[step]
        held = outs[which].at[rows_of(row + stays, length), pl.ds(col, unit_cols)]
        return pltpu.make_async_remote_copy(
            src_ref=held,
            dst_ref=held,
            send_sem=back_send.at[step, unit],
            recv_sem=back_recv.at[step, unit],
            device_id={"ctx": other(order(turn)[step])},
            device_id_type=MESH,
        )

    def add(left, right):
        return (left.astype(jnp.float32) + right.astype(jnp.float32)).astype(jnp.bfloat16)

    def launch(which, unit, turn, row, col):
        here(which, unit, row, col).start()
        across(which, unit, row, col).start()

    def first(which, unit, turn, row, col):
        here(which, unit, row, col).wait()
        across(which, unit, row, col).wait_recv()
        own[unit] = add(own[unit], far[unit])
        scatter(0, unit, turn).start()

    def middle(step, which, unit, turn, row, col):
        scatter(step, unit, turn).wait_recv()
        stays, goes, length = cuts(turn)[step]
        arrived = near[unit, pl.ds(unit_rows - 2 * length, length)]
        if step == 0:
            total = add(own[unit, rows_of(stays, length)], arrived)
        else:
            total = add(kept[unit, rows_of(stays - cuts(turn)[0][0], length)], arrived)
        if step < steps - 1:
            kept[unit, rows_of(stays - cuts(turn)[0][0], length)] = total
            scatter(step + 1, unit, turn).start()
        else:
            outs[which][rows_of(row + stays, length), pl.ds(col, unit_cols)] = total
            gather(step, which, unit, turn, row, col).start()

    def spread(step, which, unit, turn, row, col):
        gather(step, which, unit, turn, row, col).wait_recv()
        if step > 0:
            gather(step - 1, which, unit, turn, row, col).start()

    def finish(which, unit, turn, row, col):
        across(which, unit, row, col).wait_send()
        for step in range(steps):
            scatter(step, unit, turn).wait_send()
            gather(step, which, unit, turn, row, col).wait_send()

    stages = [launch, first]
    stages += [functools.partial(middle, step) for step in range(steps)]
    stages += [functools.partial(spread, step) for step in reversed(range(steps))]
    stages += [finish]
    return [functools.partial(each, stage) for stage in stages]


def sum_kernel(sizes, ways, unit_cols, *refs):
    for stage in sum_plan(sizes, ways, unit_cols, refs):
        stage()


def sum_attend_kernel(sizes, ways, unit_cols, rows, *refs):
    count = len(sizes)
    query_ref, query_t_ref, key_ref, key_t_ref, value_ref, grad_ref, grad_t_ref = refs[:7]
    log_ref, delta_ref = refs[7:9]
    parts = refs[9 : 9 + count]
    query_grad_ref, key_grad_ref, value_grad_ref = refs[9 + count : 12 + count]
    outs = refs[12 + count : 12 + 2 * count]
    query_acc = refs[12 + 2 * count]
    stages = sum_plan(sizes, ways, unit_cols, (*parts, *outs, *refs[13 + 2 * count :]))
    stages[0]()
    shares = 4
    tasks = [stages[1]]
    tasks += [functools.partial(stage, share, shares) for stage in stages[2:-1] for share in range(shares)]
    tasks += [stages[-1]]
    blocks = query_t_ref.shape[1] // rows
    query_acc[...] = jnp.zeros_like(query_acc)

    def column(at, carry):
        start = pl.multiple_of(at * rows, rows)
        own = pl.ds(start, rows)

        def advance(block, kept, masked):
            key_sum, value_sum = kept
            first = pl.multiple_of(block * rows, rows)
            part = pl.ds(first, rows)
            scores = dot(key_ref[own, :], query_t_ref[:, part])
            probs = jnp.exp(scores - log_ref[:, part])
            if masked:
                probs = jnp.where(diagonal(rows), probs, 0.0)
            prob_grad = dot(value_ref[own, :], grad_t_ref[:, part])
            score_grad = (probs * (prob_grad - delta_ref[:, part])).astype(jnp.bfloat16)
            value_sum = value_sum + dot(probs.astype(jnp.bfloat16), grad_ref[part, :])
            key_sum = key_sum + dot(score_grad, query_ref[part, :])
            query_acc[:, part] += dot(key_t_ref[:, own], score_grad)
            return key_sum, value_sum

        zero = jnp.zeros((rows, HEAD_DIM), jnp.float32)
        state = advance(at, (zero, zero), True)
        key_sum, value_sum = lax.fori_loop(
            at + 1, blocks, lambda block, kept: advance(block, kept, False), state
        )
        key_grad_ref[own, :] = key_sum.astype(jnp.bfloat16)
        value_grad_ref[own, :] = value_sum.astype(jnp.bfloat16)
        for turn, task in enumerate(tasks[:blocks]):
            pl.when(at == turn)(task)
        return carry

    lax.fori_loop(0, blocks, column, 0)
    query_grad_ref[...] = (query_acc[...] * HEAD_DIM**-0.5).astype(jnp.bfloat16)
    for task in tasks[blocks:]:
        task()


def unit_columns(parts):
    return math.gcd(1024, *[part.shape[1] for part in parts])


def can_sum(parts):
    ways, cores = lax.axis_size("ctx"), lax.axis_size("seq")
    if cores != 2 or ways < 4 or ways & (ways - 1):
        return False
    for part in parts:
        rows = part.shape[0] // cores
        if rows % (UNIT_ROWS * ways):
            return False
    return True


def sum_scratch(sizes, ways, unit_cols):
    unit = (UNIT_ROWS * ways, unit_cols)
    units = sum(rows * cols for rows, cols in sizes) // (unit[0] * unit[1])
    steps = ways.bit_length() - 1
    bf16, dma = jnp.bfloat16, pltpu.SemaphoreType.DMA
    return [
        pltpu.VMEM((units, *unit), bf16),
        pltpu.VMEM((units, *unit), bf16),
        pltpu.VMEM((units, *unit), bf16),
        pltpu.VMEM((units, unit[0] // 2, unit[1]), bf16),
        dma((units,)),
        dma((units,)),
        dma((units,)),
        dma((steps, units)),
        dma((steps, units)),
        dma((steps, units)),
        dma((steps, units)),
    ]


def total_grads(call, parts):
    if not can_sum(parts):
        return [total_grad(part) for part in parts]
    ways = lax.axis_size("ctx")
    unit_cols = unit_columns(parts)
    sizes = [(part.shape[0] // 2, part.shape[1]) for part in parts]
    sums = pl.pallas_call(
        functools.partial(sum_kernel, sizes, ways, unit_cols),
        in_specs=[pl.BlockSpec(memory_space=pl.ANY)] * len(parts),
        out_specs=[pl.BlockSpec(memory_space=pltpu.VMEM)] * len(parts),
        out_shape=[jax.ShapeDtypeStruct(size, jnp.bfloat16) for size in sizes],
        scratch_shapes=sum_scratch(sizes, ways, unit_cols),
        compiler_params=pltpu.CompilerParams(
            collective_id=call, has_side_effects=True, vmem_limit_bytes=56 * 2**20
        ),
    )(*[part.astype(jnp.bfloat16) for part in parts])
    return [item.astype(jnp.float32) for item in sums]


def attend_back_sum(call, operands, parts, rows):
    ways = lax.axis_size("ctx")
    unit_cols = unit_columns(parts)
    sizes = [(part.shape[0] // 2, part.shape[1]) for part in parts]
    operands = [item[0] for item in operands]
    length, features = operands[0].shape
    bf16 = jnp.bfloat16
    vmem = pl.BlockSpec(memory_space=pltpu.VMEM)
    query_grad, key_grad, value_grad, *sums = pl.pallas_call(
        functools.partial(sum_attend_kernel, sizes, ways, unit_cols, rows),
        in_specs=[vmem] * len(operands) + [pl.BlockSpec(memory_space=pl.ANY)] * len(parts),
        out_specs=[vmem] * (3 + len(parts)),
        out_shape=[
            jax.ShapeDtypeStruct((features, length), bf16),
            jax.ShapeDtypeStruct((length, features), bf16),
            jax.ShapeDtypeStruct((length, features), bf16),
            *[jax.ShapeDtypeStruct(size, bf16) for size in sizes],
        ],
        scratch_shapes=[
            pltpu.VMEM((features, length), jnp.float32),
            *sum_scratch(sizes, ways, unit_cols),
        ],
        compiler_params=pltpu.CompilerParams(
            collective_id=call, has_side_effects=True, vmem_limit_bytes=60 * 2**20
        ),
    )(*operands, *[part.astype(bf16) for part in parts])
    grads = [query_grad[None], key_grad.T[None], value_grad.T[None]]
    return grads, [item.astype(jnp.float32) for item in sums]


def local(
    layer_input,
    ln1_gain,
    ln1_bias,
    qkv_weight,
    query_bias,
    value_bias,
    out_weight,
    out_bias,
    ln2_gain,
    ln2_bias,
    up_weight,
    up_bias,
    down_weight,
    down_bias,
    out_cotangent,
):
    small = (
        ln1_gain,
        ln1_bias,
        query_bias,
        value_bias,
        out_bias,
        ln2_gain,
        ln2_bias,
        up_bias,
        down_bias,
    )
    sizes = [item.shape[0] for item in small]
    cuts = [sum(sizes[: at + 1]) for at in range(len(sizes) - 1)]
    small_full = lax.all_gather(jnp.concatenate(small), "seq", axis=0)
    (gain_one, shift_one, q_bias, v_bias, o_bias, gain_two, shift_two, u_bias, d_bias) = [
        item.reshape(-1) for item in jnp.split(small_full, cuts, axis=1)
    ]
    qkv_full = lax.all_gather(qkv_weight, "seq", axis=0, tiled=True)
    out_full = lax.all_gather(out_weight, "seq", axis=0, tiled=True)
    up_full = lax.all_gather(up_weight, "seq", axis=0, tiled=True)
    down_full = lax.all_gather(down_weight, "seq", axis=0, tiled=True)
    seq_count, block_len, model_width = layer_input.shape
    f32 = jnp.float32
    bf16 = jnp.bfloat16
    input_f32 = layer_input.astype(f32)
    gain_one_f = gain_one.astype(f32)
    shift_one_f = shift_one.astype(f32)
    gain_two_f = gain_two.astype(f32)
    shift_two_f = shift_two.astype(f32)
    normed_one = layer_norm(input_f32, gain_one_f, shift_one_f).astype(bf16)
    projected = jnp.einsum("std,de->ste", normed_one, qkv_full, preferred_element_type=f32)
    queries = (projected[..., :model_width] + q_bias.astype(f32)).astype(bf16)
    keys = projected[..., model_width : 2 * model_width].astype(bf16)
    values = (projected[..., 2 * model_width :] + v_bias.astype(f32)).astype(bf16)
    by_heads = HEADS % lax.axis_size("ctx") == 0
    if by_heads:
        attention_low, kept_heads = head_forward(queries, keys, values)
    else:
        attention, log_total = block_forward(queries, keys, values)
        attention_low = attention.astype(bf16)
    mid = (
        input_f32
        + jnp.einsum("std,de->ste", attention_low, out_full, preferred_element_type=f32)
        + o_bias.astype(f32)
    )
    normed_two = layer_norm(mid, gain_two_f, shift_two_f).astype(bf16)
    hidden = jnp.einsum(
        "std,df->stf", normed_two, up_full, preferred_element_type=f32
    ) + u_bias.astype(f32)
    activated = jax.nn.gelu(hidden).astype(bf16)
    result = (
        mid
        + jnp.einsum("stf,fd->std", activated, down_full, preferred_element_type=f32)
        + d_bias.astype(f32)
    )
    layer_output = result.astype(bf16)
    cotangent_f = out_cotangent.astype(f32)
    down_bias_grad = jnp.sum(cotangent_f, axis=(0, 1))
    down_weight_grad = jnp.einsum(
        "stf,std->fd", activated, out_cotangent, preferred_element_type=f32
    )
    act_grad = jnp.einsum("std,fd->stf", out_cotangent, down_full, preferred_element_type=f32)
    unused_gelu, gelu_pull = jax.vjp(jax.nn.gelu, hidden)
    hidden_grad = gelu_pull(act_grad)[0].astype(bf16)
    up_bias_grad = jnp.sum(hidden_grad.astype(f32), axis=(0, 1))
    up_weight_grad = jnp.einsum("std,stf->df", normed_two, hidden_grad, preferred_element_type=f32)
    normed_two_grad = jnp.einsum("stf,df->std", hidden_grad, up_full, preferred_element_type=f32)
    unused_two, norm_two_pull = jax.vjp(layer_norm, mid, gain_two_f, shift_two_f)
    mid_norm_grad, ln2_gain_grad, ln2_bias_grad = norm_two_pull(normed_two_grad)
    mid_grad = cotangent_f + mid_norm_grad
    branch_grad = mid_grad.astype(bf16)
    out_bias_grad = jnp.sum(branch_grad.astype(f32), axis=(0, 1))
    out_weight_grad = jnp.einsum(
        "std,ste->de", attention_low, branch_grad, preferred_element_type=f32
    )
    attention_grad = jnp.einsum(
        "ste,de->std", branch_grad, out_full, preferred_element_type=f32
    ).astype(bf16)
    if by_heads:
        (query_low, key_low, value_low), (up_sum, down_sum) = head_backward(
            kept_heads, attention_grad, [up_weight_grad, down_weight_grad]
        )
    else:
        query_low, key_low, value_low = block_backward(
            queries, keys, values, attention, log_total, attention_grad
        )
        up_sum, down_sum = total_grads(0, [up_weight_grad, down_weight_grad])
    query_bias_grad = jnp.sum(query_low.astype(f32), axis=(0, 1))
    value_bias_grad = jnp.sum(value_low.astype(f32), axis=(0, 1))
    joined_grad = jnp.concatenate([query_low, key_low, value_low], axis=-1)
    qkv_weight_grad = jnp.einsum("std,ste->de", normed_one, joined_grad, preferred_element_type=f32)
    normed_one_grad = jnp.einsum("ste,de->std", joined_grad, qkv_full, preferred_element_type=f32)
    unused_one, norm_one_pull = jax.vjp(layer_norm, input_f32, gain_one_f, shift_one_f)
    input_norm_grad, ln1_gain_grad, ln1_bias_grad = norm_one_pull(normed_one_grad)
    input_grad = mid_grad + input_norm_grad
    small_grads = (
        ln1_gain_grad,
        ln1_bias_grad,
        query_bias_grad,
        value_bias_grad,
        out_bias_grad,
        ln2_gain_grad,
        ln2_bias_grad,
        up_bias_grad,
        down_bias_grad,
    )
    ways = lax.axis_size("seq")
    small_part = jnp.concatenate([item.reshape(ways, -1) for item in small_grads], axis=1)
    unit_size = UNIT_ROWS * lax.axis_size("ctx") * model_width
    small_part = jnp.pad(small_part, ((0, 0), (0, -small_part.shape[1] % unit_size)))
    qkv_sum, out_sum, small_sum = total_grads(
        1, [qkv_weight_grad, out_weight_grad, small_part.reshape(-1, model_width)]
    )
    small_sum = small_sum.reshape(-1)[: sum(sizes)]
    (
        ln1_gain_sum,
        ln1_bias_sum,
        query_bias_sum,
        value_bias_sum,
        out_bias_sum,
        ln2_gain_sum,
        ln2_bias_sum,
        up_bias_sum,
        down_bias_sum,
    ) = jnp.split(small_sum, cuts)
    return (
        layer_output,
        input_grad,
        ln1_gain_sum,
        ln1_bias_sum,
        qkv_sum,
        query_bias_sum,
        value_bias_sum,
        out_sum,
        out_bias_sum,
        ln2_gain_sum,
        ln2_bias_sum,
        up_sum,
        up_bias_sum,
        down_sum,
        down_bias_sum,
    )


def solution(mesh):
    return jax.shard_map(
        local,
        mesh=mesh,
        in_specs=(
            P("seq", "ctx", None),
            P("seq"),
            P("seq"),
            P("seq", None),
            P("seq"),
            P("seq"),
            P("seq", None),
            P("seq"),
            P("seq"),
            P("seq"),
            P("seq", None),
            P("seq"),
            P("seq", None),
            P("seq"),
            P("seq", "ctx", None),
        ),
        out_specs=(
            P("seq", "ctx", None),
            P("seq", "ctx", None),
            P("seq"),
            P("seq"),
            P("seq", None),
            P("seq"),
            P("seq"),
            P("seq", None),
            P("seq"),
            P("seq"),
            P("seq"),
            P("seq", None),
            P("seq"),
            P("seq", None),
            P("seq"),
        ),
        check_vma=False,
    )
```
